512 devices in a mesh: mem: 16 (over y_lo, x, core), lat: 32 (over y_hi, z).
Axes of the slice: x: 4, y: 4 (y_hi: 2, y_lo: 2; y = y_hi * 2 + y_lo), z: 16, core: 2. Of those that a mesh axis runs over, the one named last changes fastest.
Arguments:
- perturbation: bfloat16 [256, 512, 2048], P('mem', 'lat'), may hold values from -6 to 6
- obs_cells: int32 [32, 2048], P('lat'), may hold values from 0 to 32767
- obs_count: int32 [32], P('lat'), may hold values from 682 to 2048, as said below
- innovation: float32 [32, 2048], P('lat'), may hold values from -8 to 8
- obs_scale: float32 [32, 2048], P('lat'), may hold values from 0.3 to 3
Outputs:
- control: float32 [256, 256, 1024], P('mem', 'lat')
- increment: float32 [512, 2048], P('lat', 'mem')
The draws below stay inside these ranges and needn't reach their ends.
Inputs may be any that keep to these rules, and one draw needn't show every extreme that they name: `obs_count`: at most 2048 live slots in a band, and some band has exactly 2048.
All inputs are finite; a program needn't handle non-finite values.
Results may differ from the reference program's by a relative error of at most 0.00035.
Values sent between devices are 32-bit elements; how exact they have to be, the bound alone decides.
A program may use at most 64 MiB of HBM per device.

```python
import math
import jax
import jax.numpy as jnp
from jax import lax

MEM_DEV = 16
MEMBERS = 256
FROWS = 16
NLON = 2048
HALO = 8
LSIG = 3
OBS = 2048
ITERS = 3
BANDS = 32
NFR = 512
NCR = 256
NLONC = 1024
N_MEM = 16


def draw_obs_count(key, part):
    base = jax.random.fold_in(key, 11)
    count_key, band_key = jax.random.split(base)
    counts = jax.random.randint(count_key, (BANDS,), OBS // 3, OBS + 1)
    full_band = jax.random.randint(band_key, (), 0, BANDS)
    return jnp.where(jnp.arange(BANDS) == full_band, OBS, counts).astype(jnp.int32)


def set_ends(values, key, smallest, largest):
    dims = values.shape
    place = [jax.random.randint(jax.random.fold_in(key, axis), (), 0, dims[axis]) for axis in range(len(dims))]
    values = values.at[tuple(place)].set(smallest)
    longest = dims.index(max(dims))
    place[longest] = (place[longest] + 1) % dims[longest]
    return values.at[tuple(place)].set(largest)


def steps_of(key, shape, cuts, low, top_value):
    loudness = 1.0
    for position, parts in cuts:
        draws = jax.random.uniform(jax.random.fold_in(jax.random.fold_in(key, 6), position), (parts,), jnp.float32, low / len(cuts), top_value / len(cuts))
        loudness = loudness * jnp.repeat(jnp.exp(draws), shape[position] // parts).reshape((-1,) + (1,) * (len(shape) - 1 - position))
    return loudness


def noise(own_key, shape, deviation, most, cuts=(), held_as=jnp.bfloat16):
    result = deviation * jax.random.normal(own_key, shape, jnp.float32)
    if cuts:
        result = result * steps_of(own_key, shape, cuts, -0.22, 0.18)
    return jnp.clip(result, -most, most).astype(held_as)


def setup_inputs(seed: int = 0) -> dict:
    arg_keys = jax.random.split(jax.random.key(seed), 6)
    return {
        "perturbation": noise(arg_keys[0], (MEMBERS, NFR, NLON), 1.0, 6.0, ((0, 16), (1, 32))),
        "obs_cells": set_ends(jax.random.randint(arg_keys[1], (BANDS, OBS), 0, FROWS * NLON), jax.random.fold_in(arg_keys[1], 1), 0, (FROWS * NLON) - 1).astype(jnp.int32),
        "obs_count": draw_obs_count(jax.random.fold_in(arg_keys[5], 71), 0),
        "innovation": noise(arg_keys[3], (BANDS, OBS), 2.0, 8.0, ((0, 32),), jnp.float32),
        "obs_scale": jnp.clip(jnp.exp(math.log(3.0) - 2.3025851 * jax.random.uniform(arg_keys[4], (BANDS, OBS), jnp.float32) ** steps_of(arg_keys[4], (BANDS, OBS), ((0, 32),), -0.2, 0.2)), 0.3, 3.0),
    }


def lat_weights():
    offsets = jnp.arange(2 * HALO + 1).astype(jnp.float32) - HALO
    spread = HALO / 2.0
    return 0.5 * jnp.exp(-offsets * offsets / (2.0 * spread * spread))


def lon_weights(coarse_cols):
    columns = jnp.arange(coarse_cols).astype(jnp.int32)
    distance = jnp.abs(columns[:, None] - columns[None, :])
    distance = jnp.minimum(distance, coarse_cols - distance).astype(jnp.float32)
    return jnp.exp(-distance * distance / (2.0 * LSIG * LSIG))


def lat_apply(padded, row_count, lat_taps):
    filtered = lat_taps[0] * padded[:, 0:row_count]
    for offset in range(1, 2 * HALO + 1):
        filtered = filtered + lat_taps[offset] * padded[:, offset:offset + row_count]
    return filtered


def widen_lon(coarse):
    odd_part = 0.5 * (coarse + jnp.roll(coarse, -1, axis=-1))
    return jnp.stack([coarse, odd_part], axis=-1).reshape(coarse.shape[:-1] + (2 * coarse.shape[-1],))


def narrow_lon(fine):
    paired = fine.reshape(fine.shape[:-1] + (fine.shape[-1] // 2, 2))
    odd_part = paired[..., 1]
    return paired[..., 0] + 0.5 * odd_part + 0.5 * jnp.roll(odd_part, 1, axis=-1)


def reference(perturbation, obs_cells, obs_count, innovation, obs_scale):
    lat_taps = lat_weights()
    circulant = lon_weights(NLONC)
    member_scale = (MEMBERS - 1) ** -0.5
    groups = perturbation.reshape(N_MEM, MEM_DEV, NFR, NLON)

    def forward(direction):
        padded = jnp.pad(direction, ((0, 0), (HALO, HALO), (0, 0)))
        smoothed = lat_apply(padded, NCR, lat_taps).reshape(N_MEM, MEM_DEV, NCR, NLONC)

        def accumulate(running, block):
            smooth_block, pert_block = block
            along = jnp.dot(smooth_block, circulant, precision=lax.Precision.HIGHEST, preferred_element_type=jnp.float32)
            fine_block = jnp.repeat(widen_lon(along), 2, axis=1)
            return running + jnp.sum(pert_block.astype(jnp.float32) * fine_block, axis=0) * member_scale, None

        image_field, unused = lax.scan(accumulate, jnp.zeros((NFR, NLON), jnp.float32), (smoothed, groups))
        return image_field

    def adjoint(obs_field):
        def fold(pert_block):
            weighted = pert_block.astype(jnp.float32) * obs_field[None] * member_scale
            folded = narrow_lon(weighted.reshape(MEM_DEV, NCR, 2, NLON).sum(axis=2))
            return jnp.dot(folded, circulant, precision=lax.Precision.HIGHEST, preferred_element_type=jnp.float32)

        coarse = lax.map(fold, groups).reshape(MEMBERS, NCR, NLONC)
        padded = jnp.pad(coarse, ((0, 0), (HALO, HALO), (0, 0)))
        return lat_apply(padded, NCR, lat_taps)

    band_start = (jnp.arange(BANDS).astype(jnp.int32) * (FROWS * NLON))[:, None]
    flat_index = (obs_cells.astype(jnp.int32) + band_start).reshape(-1)
    active = (jnp.arange(OBS).astype(jnp.int32)[None, :] < obs_count[:, None]).reshape(-1)
    target = innovation.reshape(-1)
    saturation = obs_scale.reshape(-1)
    control = jnp.zeros((MEMBERS, NCR, NLONC), jnp.float32)
    increment = jnp.zeros((NFR, NLON), jnp.float32)
    observed = jnp.zeros((BANDS * OBS,), jnp.float32)
    for iteration in range(ITERS):
        misfit = target - observed
        bounded = jnp.tanh(misfit / saturation)
        pull = jnp.where(active, saturation * bounded, 0.0)
        weight = jnp.where(active, 1.0 - bounded * bounded, 0.0)
        obs_field = jnp.zeros((NFR * NLON,), jnp.float32).at[flat_index].add(pull).reshape(NFR, NLON)
        gradient = control - adjoint(obs_field)
        grad_norm = jnp.sum(gradient * gradient)
        direction = -gradient
        image_field = forward(direction)
        hits = image_field.reshape(-1)[flat_index]
        bending = jnp.sum(weight * hits * hits)
        step_size = grad_norm / (grad_norm + bending + 1e-6)
        control = control + step_size * direction
        increment = increment + step_size * image_field
        observed = observed + step_size * hits
    return control, increment
```

```python
import functools

import jax
import jax.numpy as jnp
import ml_dtypes
import numpy as np
from jax import lax
from jax.experimental import pallas as pl
from jax.experimental.pallas import tpu as pltpu
from jax.sharding import PartitionSpec as P

HALO = 8
LSIG = 3
ITERS = 3
NEAR = 5
BLOCK = 256
PAD = 128
F32 = jnp.float32
BF16 = jnp.bfloat16
MESH = pl.DeviceIdType.MESH


def window_matrices(coarse_cols):
    columns = np.arange(coarse_cols)
    distance = np.minimum(columns, coarse_cols - columns).astype(np.float32)
    first = np.exp(-distance * distance / np.float32(2.0 * LSIG * LSIG)).astype(np.float64)
    circulant = first[np.abs(columns[:, None] - columns[None, :])]
    squared = first @ circulant
    apart = np.arange(BLOCK + 2 * PAD)[:, None] - PAD - np.arange(BLOCK)[None, :]
    parts = []
    for row in (first, squared):
        inside = np.abs(apart) < min(PAD, coarse_cols // 2)
        window = np.where(inside, row[np.abs(apart) % coarse_cols], 0.0).astype(np.float32)
        high = window.astype(ml_dtypes.bfloat16)
        parts += [high, (window - high.astype(np.float32)).astype(ml_dtypes.bfloat16)]
    return np.stack(parts)


def widen_matrix():
    fine = np.arange(256) * 0.5
    coarse = np.arange(256)
    return np.maximum(0.0, 1.0 - np.abs(coarse[:, None] - fine[None, :])).astype(
        ml_dtypes.bfloat16
    )


def split_rows_matrix(members, rows):
    matrix = np.zeros((members * rows, members * rows), ml_dtypes.bfloat16)
    for member in range(members):
        for row in range(rows):
            to = (row % 2) * members * (rows // 2) + member * (rows // 2) + row // 2
            matrix[to, member * rows + row] = 1.0
    return matrix


def halves(value):
    high = value.astype(BF16)
    return high, (value - high.astype(F32)).astype(BF16)


def dot(a, b):
    return jnp.dot(a, b, preferred_element_type=F32)


def body(
    n_mem,
    n_lat,
    cells_ref,
    count_ref,
    innov_ref,
    scale_ref,
    pert_ref,
    sel_ref,
    win_ref,
    widen_ref,
    control_ref,
    inc_ref,
    meta,
    bvals,
    spread,
    chosen,
    picked,
    onehot,
    filt,
    filt2,
    target,
    scale,
    live,
    observed,
    summed,
    q_now,
    weight,
    acc,
    vext,
    vwide,
    along,
    image,
    image_acc,
    hsend,
    hrecv,
    hnear,
    ssend,
    srecv,
    irecv,
    meta_send,
    meta_recv,
    b_send,
    b_recv,
    h_send,
    h_recv,
    n_send,
    n_recv,
    s_send,
    s_recv,
    i_send,
    i_recv,
):
    members, fine_rows, fine_cols = pert_ref.shape
    rows, cols = fine_rows // 2, fine_cols // 2
    slots = cells_ref.shape[1]
    flat = members * rows
    c = float((members * n_mem - 1) ** -0.5)
    mem = lax.axis_index("mem")
    lat = lax.axis_index("lat")
    barrier = pltpu.get_barrier_semaphore()

    def mem_peer(r):
        return {"mem": lax.rem(mem + r, n_mem)}

    def lat_peer(r):
        return {"lat": lax.rem(lat + r, n_lat)}

    def offset(n):
        return ((n + 1) // 2) * (1 - 2 * (n % 2))

    def remote(src, dst, send, recv, device):
        return pltpu.make_async_remote_copy(
            src_ref=src,
            dst_ref=dst,
            send_sem=send,
            recv_sem=recv,
            device_id=device,
            device_id_type=MESH,
        )

    def wait_all(ref, sem):
        pltpu.make_async_copy(ref, ref, sem).wait()

    @pl.loop(1, n_mem)
    def _(r):
        pl.semaphore_signal(barrier, inc=1, device_id=mem_peer(r), device_id_type=MESH)

    @pl.loop(1, n_lat)
    def _(r):
        pl.semaphore_signal(barrier, inc=1, device_id=lat_peer(r), device_id_type=MESH)

    cells = cells_ref[...]
    row = cells >> (fine_cols.bit_length() - 1)
    col = cells & (fine_cols - 1)
    coarse_row = (row >> 1).astype(F32)
    slot_id = lax.broadcasted_iota(jnp.int32, (1, slots), 1)
    meta[0, 0:1, :] = col.astype(F32) * 0.5
    meta[0, 1:2, :] = coarse_row
    meta[0, 2:3, :] = innov_ref[...]
    meta[0, 3:4, :] = scale_ref[...]
    meta[0, 4:5, :] = jnp.where(slot_id < count_ref[0], 1.0, 0.0)
    meta[0, 5:6, :] = col.astype(F32)
    meta[0, 6:7, :] = (row & 1).astype(F32)
    meta[0, 7:8, :] = jnp.zeros((1, slots), F32)
    pl.semaphore_wait(barrier, n_mem + n_lat - 2)

    def near_peer(n):
        return {"lat": lax.rem(lat - offset(n) + n_lat, n_lat)}

    def meta_copy(n):
        return remote(
            meta.at[0], meta.at[n], meta_send.at[n - 1], meta_recv.at[n - 1], near_peer(n)
        )

    def value_copy(n):
        return remote(
            bvals.at[0], bvals.at[n], b_send.at[n - 1], b_recv.at[n - 1], near_peer(n)
        )

    @pl.loop(1, NEAR)
    def _(n):
        meta_copy(n).start()

    @pl.loop(0, fine_cols // BLOCK)
    def _(j):
        at = pl.ds(pl.multiple_of(j * BLOCK, BLOCK), BLOCK)
        picked[:, at] = dot(
            sel_ref[...], pert_ref[:, :, at].reshape(members * fine_rows, BLOCK)
        ).astype(BF16)

    @pl.loop(0, slots // BLOCK)
    def _(j):
        at = pl.ds(pl.multiple_of(j * BLOCK, BLOCK), BLOCK)
        column = meta[0, 5:6, at]
        place = lax.broadcasted_iota(jnp.int32, (fine_cols, BLOCK), 0).astype(F32)
        hit = jnp.where(place == column, 1.0, 0.0).astype(BF16)
        both = dot(picked[...], hit)
        value = jnp.where(meta[0, 6:7, at] > 0.5, both[flat:], both[:flat])
        own = lax.broadcasted_iota(jnp.int32, (rows, BLOCK), 0).astype(F32) == meta[0, 1:2, at]
        value = jnp.where(own[None], value.reshape(members, rows, BLOCK), 0.0)
        chosen[:, at] = value.reshape(flat, BLOCK).astype(BF16)
        bvals[0, :, at] = jnp.sum(value, axis=1)

    @pl.loop(1, NEAR)
    def _(n):
        value_copy(n).start()

    target[...] = jnp.zeros_like(target)
    scale[...] = jnp.ones_like(scale)
    live[...] = jnp.zeros_like(live)
    observed[...] = jnp.zeros_like(observed)
    summed[...] = jnp.zeros_like(summed)

    @pl.loop(0, NEAR)
    def _(n):
        @pl.when(n > 0)
        def _():
            meta_copy(n).wait_recv()

        x = meta[n, 0:1, :]
        step = 128

        @pl.loop(0, cols // step)
        def _(j):
            start = pl.multiple_of(j * step, step)
            place = (lax.broadcasted_iota(jnp.int32, (step, slots), 0) + start).astype(F32)
            hat = jnp.maximum(1.0 - jnp.abs(x - place), 0.0)
            onehot[n, pl.ds(start, step), :] = hat.astype(BF16)

        place = lax.broadcasted_iota(jnp.int32, (16, slots), 0).astype(F32)
        hat = jnp.maximum(
            jnp.maximum(1.0 - jnp.abs(x - place), 1.0 - jnp.abs(x - (place + float(cols)))), 0.0
        )
        onehot[n, 0:16, :] = hat.astype(BF16)

        reach = rows + 2 * HALO
        between = lax.broadcasted_iota(jnp.int32, (reach, slots), 0) - HALO
        whole = between + lat * rows
        there = meta[n, 1:2, :] + (offset(n) * rows).astype(F32)
        apart = between.astype(F32) - there
        spread_sq = 2.0 * (HALO / 2.0) ** 2
        taps = jnp.where(
            (jnp.abs(apart) <= HALO) & (whole >= 0) & (whole < n_lat * rows),
            (0.5 * c) * jnp.exp(-apart * apart / spread_sq),
            0.0,
        )
        filt[n] = taps[HALO : HALO + rows]
        own = lax.broadcasted_iota(jnp.int32, (rows, reach), 0).astype(F32)
        middle = lax.broadcasted_iota(jnp.int32, (rows, reach), 1).astype(F32) - HALO
        away = middle - own
        first = jnp.where(jnp.abs(away) <= HALO, 0.5 * jnp.exp(-away * away / spread_sq), 0.0)
        filt2[n] = jnp.dot(
            first, taps, precision=lax.Precision.HIGHEST, preferred_element_type=F32
        )
        band = lat + offset(n)
        inside = jnp.where((band >= 0) & (band < n_lat), 1.0, 0.0)
        target[pl.ds(n, 1), :] = meta[n, 2:3, :]
        scale[pl.ds(n, 1), :] = meta[n, 3:4, :]
        live[pl.ds(n, 1), :] = meta[n, 4:5, :] * inside

    image_acc[...] = jnp.zeros_like(image_acc)
    control_ref[...] = jnp.zeros_like(control_ref)

    def scattered(filter_ref, bands, first):
        acc[...] = jnp.zeros_like(acc)

        @pl.loop(0, bands)
        def _(n):
            @pl.when(first & (n > 0))
            def _():
                value_copy(n).wait_recv()

            @pl.when(first)
            def _():
                values = jnp.broadcast_to(bvals[n][:, None, :], (members, rows, slots))
                spread[n] = values.reshape(flat, slots).astype(BF16)

            factor = filter_ref[n] * q_now[pl.ds(n, 1), :]
            value = spread[n].astype(F32).reshape(members, rows, slots) * factor[None]
            high, low = halves(value.reshape(flat, slots))
            acc[...] += lax.dot_general(
                jnp.concatenate([high, low], axis=0),
                onehot[n],
                (((1,), (1,)), ((), ())),
                preferred_element_type=F32,
            )

        return acc[:flat] + acc[flat:]

    def filtered(value, which):
        high, low = halves(value)
        both = jnp.concatenate([high, low], axis=0)
        vext[:, PAD : PAD + cols] = both
        vext[:, :PAD] = both[:, cols - PAD :]
        vext[:, PAD + cols :] = both[:, :PAD]
        blocks = []
        for j in range(cols // BLOCK):
            window = vext[:, j * BLOCK : j * BLOCK + BLOCK + 2 * PAD]
            product = dot(window, win_ref[2 * which])
            blocks.append(
                product[:flat] + product[flat:] + dot(window[:flat], win_ref[2 * which + 1])
            )
        return blocks

    def send_image(k):
        @pl.loop(1, n_mem)
        def _(r):
            to = lax.rem(mem + r, n_mem)
            width = inc_ref.shape[1]
            part = pl.ds(pl.multiple_of(to * width, 128), width)
            remote(
                image.at[k, :, part], irecv.at[k, r - 1], i_send.at[k], i_recv.at[k], mem_peer(r)
            ).start()

    @pl.loop(0, ITERS)
    def _(t):
        last = t == ITERS - 1
        bounded = jnp.tanh((target[...] - observed[...]) / scale[...])
        q_now[...] = live[...] * (scale[...] * bounded) - summed[...]
        weight[...] = (live[...] * (1.0 - bounded * bounded))[0:1]

        for j, block in enumerate(filtered(scattered(filt2, NEAR, t == 0), 1)):
            high, low = halves(block)
            vwide[:, j * BLOCK : (j + 1) * BLOCK] = jnp.concatenate([high, low], axis=0)
        vwide[:, cols:] = vwide[:, :PAD]

        seen = dot(vwide[:, :cols], onehot[0])
        hits_part = c * jnp.sum(
            chosen[...].astype(F32) * (seen[:flat] + seen[flat:]), axis=0, keepdims=True
        )
        hsend[t] = hits_part

        @pl.loop(1, n_mem)
        def _(r):
            remote(
                hsend.at[t], hrecv.at[t, r - 1], h_send.at[t], h_recv.at[t], mem_peer(r)
            ).start()

        at_t = jnp.where(last, 1, 0)
        for j in range(fine_cols // 256):
            wide = dot(vwide[:, 128 * j : 128 * j + 256], widen_ref[...])
            wide = (wide[:flat] + wide[flat:]).reshape(members, rows, 256)
            here = slice(256 * j, 256 * (j + 1))
            for e in range(2):
                pert = picked[e * flat : (e + 1) * flat, here].astype(F32)
                total = c * jnp.sum(pert.reshape(members, rows, 256) * wide, axis=0)
                image[at_t, e * rows : (e + 1) * rows, here] = total

        @pl.when(last)
        def _():
            send_image(1)

        wait_all(hrecv.at[t], h_recv.at[t])
        hits = hits_part + jnp.sum(hrecv[t], axis=0)
        q_own = q_now[0:1, :]
        gg_part = q_own * hits
        cc_part = weight[...] * hits * hits
        width = 128
        ssend[t, :, :width] = sum(
            gg_part[:, i : i + width] for i in range(0, slots, width)
        )
        ssend[t, :, width:] = sum(
            cc_part[:, i : i + width] for i in range(0, slots, width)
        )

        @pl.loop(1, n_lat)
        def _(r):
            remote(
                ssend.at[t], srecv.at[t, r - 1], s_send.at[t], s_recv.at[t], lat_peer(r)
            ).start()

        hnear[t, 0] = hits

        def near_hits(n):
            return remote(
                hnear.at[t, 0],
                hnear.at[t, n],
                n_send.at[t, n - 1],
                n_recv.at[t, n - 1],
                near_peer(n),
            )

        @pl.loop(1, NEAR)
        def _(n):
            near_hits(n).start()

        for j, block in enumerate(filtered(scattered(filt, 3, t < 0), 0)):
            along[:, j * BLOCK : (j + 1) * BLOCK] = block

        wait_all(srecv.at[t], s_recv.at[t])
        sums = ssend[t] + jnp.sum(srecv[t], axis=0)
        gg = jnp.maximum(jnp.sum(sums[:, :width], axis=1, keepdims=True), 0.0)
        cc = jnp.sum(sums[:, width:], axis=1, keepdims=True)
        step = gg / (gg + cc + 1e-6)

        control_ref[...] += step[None] * along[...].reshape(members, rows, cols)
        summed[...] += step * q_now[...]
        observed[0:1, :] += step * hits

        @pl.loop(1, NEAR)
        def _(n):
            near_hits(n).wait_recv()
            observed[pl.ds(n, 1), :] += step * hnear[t, n]

        @pl.when(jnp.logical_not(last))
        def _():
            image_acc[...] += step * image[0]

        @pl.when(t == ITERS - 2)
        def _():
            image[0] = image_acc[...]
            send_image(0)

        @pl.when(last)
        def _():
            width = inc_ref.shape[1]
            part = pl.ds(pl.multiple_of(mem * width, 128), width)
            wait_all(irecv.at[0], i_recv.at[0])
            wait_all(irecv.at[1], i_recv.at[1])
            before = image[0, :, part] + jnp.sum(irecv[0], axis=0)
            now = image[1, :, part] + jnp.sum(irecv[1], axis=0)
            total = before + step * now
            for e in range(2):
                inc_ref[pl.ds(e, rows, 2), :] = total[e * rows : (e + 1) * rows]

    @pl.loop(1, NEAR)
    def _(n):
        meta_copy(n).wait_send()
        value_copy(n).wait_send()

    @pl.loop(0, ITERS)
    def _(t):
        wait_all(hrecv.at[t], h_send.at[t])
        wait_all(srecv.at[t], s_send.at[t])

        @pl.loop(1, NEAR)
        def _(n):
            wait_all(hnear.at[t, n], n_send.at[t, n - 1])

    wait_all(irecv.at[0], i_send.at[0])
    wait_all(irecv.at[1], i_send.at[1])


def on_device(n_mem, n_lat, windows, pert, cells, count, innov, scale):
    members, fine_rows, fine_cols = pert.shape
    rows, cols = fine_rows // 2, fine_cols // 2
    slots = cells.shape[1]
    flat = members * rows
    width = fine_cols // n_mem
    vmem = pl.BlockSpec(memory_space=pltpu.VMEM)
    scratch = [
        pltpu.VMEM((NEAR, 8, slots), F32),
        pltpu.VMEM((NEAR, members, slots), F32),
        pltpu.VMEM((NEAR, flat, slots), BF16),
        pltpu.VMEM((flat, slots), BF16),
        pltpu.VMEM((2 * flat, fine_cols), BF16),
        pltpu.VMEM((NEAR, cols, slots), BF16),
        pltpu.VMEM((NEAR, rows, slots), F32),
        pltpu.VMEM((NEAR, rows, slots), F32),
        pltpu.VMEM((8, slots), F32),
        pltpu.VMEM((8, slots), F32),
        pltpu.VMEM((8, slots), F32),
        pltpu.VMEM((8, slots), F32),
        pltpu.VMEM((8, slots), F32),
        pltpu.VMEM((8, slots), F32),
        pltpu.VMEM((1, slots), F32),
        pltpu.VMEM((2 * flat, cols), F32),
        pltpu.VMEM((2 * flat, cols + 2 * PAD), BF16),
        pltpu.VMEM((2 * flat, cols + PAD), BF16),
        pltpu.VMEM((flat, cols), F32),
        pltpu.VMEM((2, fine_rows, fine_cols), F32),
        pltpu.VMEM((fine_rows, fine_cols), F32),
        pltpu.VMEM((ITERS, 1, slots), F32),
        pltpu.VMEM((ITERS, n_mem - 1, 1, slots), F32),
        pltpu.VMEM((ITERS, NEAR, 1, slots), F32),
        pltpu.VMEM((ITERS, 1, 256), F32),
        pltpu.VMEM((ITERS, n_lat - 1, 1, 256), F32),
        pltpu.VMEM((2, n_mem - 1, fine_rows, width), F32),
    ]
    scratch += [pltpu.SemaphoreType.DMA((NEAR - 1,))] * 4
    scratch += [pltpu.SemaphoreType.DMA((ITERS,))] * 2
    scratch += [pltpu.SemaphoreType.DMA((ITERS, NEAR - 1))] * 2
    scratch += [pltpu.SemaphoreType.DMA((ITERS,))] * 2
    scratch += [pltpu.SemaphoreType.DMA((2,))] * 2
    control, increment = pl.pallas_call(
        functools.partial(body, n_mem, n_lat),
        out_shape=(
            jax.ShapeDtypeStruct((members, rows, cols), F32),
            jax.ShapeDtypeStruct((fine_rows, width), F32),
        ),
        in_specs=[vmem, pl.BlockSpec(memory_space=pltpu.SMEM)] + [vmem] * 6,
        out_specs=(vmem, vmem),
        scratch_shapes=scratch,
        compiler_params=pltpu.CompilerParams(
            collective_id=0, has_side_effects=True, vmem_limit_bytes=60 * 2**20
        ),
    )(
        cells,
        count,
        innov,
        scale,
        pert,
        jnp.asarray(split_rows_matrix(members, fine_rows)),
        jnp.asarray(windows),
        jnp.asarray(widen_matrix()),
    )
    return control, increment


def solution(mesh):
    n_mem, n_lat = mesh.shape["mem"], mesh.shape["lat"]

    def run(pert, cells, count, innov, scale):
        windows = window_matrices(pert.shape[2] // 2)
        return on_device(n_mem, n_lat, windows, pert, cells, count, innov, scale)

    return jax.shard_map(
        run,
        mesh=mesh,
        in_specs=(P("mem", "lat", None), P("lat", None), P("lat"), P("lat", None), P("lat", None)),
        out_specs=(P("mem", "lat", None), P("lat", "mem")),
        check_vma=False,
    )
```

```python
import functools

import jax
import jax.numpy as jnp
import ml_dtypes
import numpy as np
from jax import lax
from jax.experimental import pallas as pl
from jax.experimental.pallas import tpu as pltpu
from jax.sharding import PartitionSpec as P

HALO = 8
LSIG = 3
ITERS = 3
NEAR = 5
BLOCK = 256
PAD = 128
F32 = jnp.float32
BF16 = jnp.bfloat16
MESH = pl.DeviceIdType.MESH


def window_matrices(coarse_cols):
    columns = np.arange(coarse_cols)
    distance = np.minimum(columns, coarse_cols - columns).astype(np.float32)
    first = np.exp(-distance * distance / np.float32(2.0 * LSIG * LSIG)).astype(np.float64)
    circulant = first[np.abs(columns[:, None] - columns[None, :])]
    squared = first @ circulant
    apart = np.arange(BLOCK + 2 * PAD)[:, None] - PAD - np.arange(BLOCK)[None, :]
    parts = []
    for row in (first, squared):
        inside = np.abs(apart) < min(PAD, coarse_cols // 2)
        window = np.where(inside, row[np.abs(apart) % coarse_cols], 0.0).astype(np.float32)
        high = window.astype(ml_dtypes.bfloat16)
        parts += [high, (window - high.astype(np.float32)).astype(ml_dtypes.bfloat16)]
    return np.stack(parts)


def widen_matrix():
    fine = np.arange(256) * 0.5
    coarse = np.arange(256)
    return np.maximum(0.0, 1.0 - np.abs(coarse[:, None] - fine[None, :])).astype(
        ml_dtypes.bfloat16
    )


def split_rows_matrix(members, rows):
    matrix = np.zeros((members * rows, members * rows), ml_dtypes.bfloat16)
    for member in range(members):
        for row in range(rows):
            to = (row % 2) * members * (rows // 2) + member * (rows // 2) + row // 2
            matrix[to, member * rows + row] = 1.0
    return matrix


def halves(value):
    high = value.astype(BF16)
    return high, (value - high.astype(F32)).astype(BF16)


def dot(a, b):
    return jnp.dot(a, b, preferred_element_type=F32)


def body(
    n_mem,
    n_lat,
    cells_ref,
    count_ref,
    innov_ref,
    scale_ref,
    pert_ref,
    sel_ref,
    win_ref,
    widen_ref,
    control_ref,
    inc_ref,
    meta,
    bvals,
    spread,
    chosen,
    picked,
    onehot,
    filt,
    filt2,
    target,
    scale,
    live,
    observed,
    summed,
    q_now,
    weight,
    acc,
    vext,
    vwide,
    along,
    image,
    image_acc,
    hsend,
    hrecv,
    hnear,
    ssend,
    srecv,
    irecv,
    meta_send,
    meta_recv,
    b_send,
    b_recv,
    h_send,
    h_recv,
    n_send,
    n_recv,
    s_send,
    s_recv,
    i_send,
    i_recv,
):
    members, fine_rows, fine_cols = pert_ref.shape
    rows, cols = fine_rows // 2, fine_cols // 2
    slots = cells_ref.shape[1]
    flat = members * rows
    c = float((members * n_mem - 1) ** -0.5)
    mem = lax.axis_index("mem")
    lat = lax.axis_index("lat")
    barrier = pltpu.get_barrier_semaphore()

    def mem_peer(r):
        return {"mem": lax.rem(mem + r, n_mem)}

    def lat_peer(r):
        return {"lat": lax.rem(lat + r, n_lat)}

    def offset(n):
        return ((n + 1) // 2) * (1 - 2 * (n % 2))

    def remote(src, dst, send, recv, device):
        return pltpu.make_async_remote_copy(
            src_ref=src,
            dst_ref=dst,
            send_sem=send,
            recv_sem=recv,
            device_id=device,
            device_id_type=MESH,
        )

    def wait_all(ref, sem):
        pltpu.make_async_copy(ref, ref, sem).wait()

    @pl.loop(1, n_mem)
    def _(r):
        pl.semaphore_signal(barrier, inc=1, device_id=mem_peer(r), device_id_type=MESH)

    @pl.loop(1, n_lat)
    def _(r):
        pl.semaphore_signal(barrier, inc=1, device_id=lat_peer(r), device_id_type=MESH)

    cells = cells_ref[...]
    slot_id = lax.broadcasted_iota(jnp.int32, (1, slots), 1)
    meta[0, 0:1, :] = cells.astype(F32)
    meta[0, 1:2, :] = innov_ref[...]
    meta[0, 2:3, :] = scale_ref[...]
    meta[0, 3:4, :] = jnp.where(slot_id < count_ref[0], 1.0, 0.0)

    def place_of(n, at):
        cell = meta[n, 0:1, at]
        fine_row = jnp.floor(cell * (1.0 / fine_cols))
        return fine_row, cell - fine_row * float(fine_cols)

    def near_peer(n):
        return {"lat": lax.rem(lat - offset(n) + n_lat, n_lat)}

    def meta_copy(n):
        return remote(
            meta.at[0], meta.at[n], meta_send.at[n - 1], meta_recv.at[n - 1], near_peer(n)
        )

    def value_copy(n):
        return remote(
            bvals.at[0], bvals.at[n], b_send.at[n - 1], b_recv.at[n - 1], near_peer(n)
        )

    @pl.loop(0, fine_cols // BLOCK)
    def _(j):
        at = pl.ds(pl.multiple_of(j * BLOCK, BLOCK), BLOCK)
        picked[:, at] = dot(
            sel_ref[...], pert_ref[:, :, at].reshape(members * fine_rows, BLOCK)
        ).astype(BF16)

    @pl.loop(0, slots // BLOCK)
    def _(j):
        at = pl.ds(pl.multiple_of(j * BLOCK, BLOCK), BLOCK)
        fine_row, column = place_of(0, at)
        coarse_row = jnp.floor(fine_row * 0.5)
        place = lax.broadcasted_iota(jnp.int32, (fine_cols, BLOCK), 0).astype(F32)
        hit = jnp.where(place == column, 1.0, 0.0).astype(BF16)
        both = dot(picked[...], hit)
        odd = fine_row - 2.0 * coarse_row
        value = jnp.where(odd > 0.5, both[flat:], both[:flat])
        own = lax.broadcasted_iota(jnp.int32, (rows, BLOCK), 0).astype(F32) == coarse_row
        value = jnp.where(own[None], value.reshape(members, rows, BLOCK), 0.0)
        chosen[:, at] = value.reshape(flat, BLOCK).astype(BF16)
        bvals[0, :, at] = jnp.sum(value, axis=1)

    target[...] = jnp.zeros_like(target)
    scale[...] = jnp.ones_like(scale)
    live[...] = jnp.zeros_like(live)
    observed[...] = jnp.zeros_like(observed)
    summed[...] = jnp.zeros_like(summed)

    def prepare(n):
        fine_row, column = place_of(n, slice(None))
        x = column * 0.5
        step = 128
        place16 = lax.broadcasted_iota(jnp.int32, (step, slots), 0).astype(F32).astype(BF16)

        @pl.loop(0, cols // step)
        def _(j):
            start = pl.multiple_of(j * step, step)
            near = jnp.clip(x - start.astype(F32), -2.0, step + 1.0).astype(BF16)
            apart = jnp.abs(near - place16)
            onehot[n, pl.ds(start, step), :] = jnp.maximum(BF16(1.0) - apart, BF16(0.0))

        place = lax.broadcasted_iota(jnp.int32, (16, slots), 0).astype(F32)
        hat = jnp.maximum(
            jnp.maximum(1.0 - jnp.abs(x - place), 1.0 - jnp.abs(x - (place + float(cols)))), 0.0
        )
        onehot[n, 0:16, :] = hat.astype(BF16)

        reach = rows + 2 * HALO
        between = lax.broadcasted_iota(jnp.int32, (reach, slots), 0) - HALO
        whole = between + lat * rows
        shift = jnp.asarray(offset(n) * rows, jnp.int32).astype(F32)
        apart = between.astype(F32) - (jnp.floor(fine_row * 0.5) + shift)
        spread_sq = 2.0 * (HALO / 2.0) ** 2
        taps = jnp.where(
            (jnp.abs(apart) <= HALO) & (whole >= 0) & (whole < n_lat * rows),
            (0.5 * c) * jnp.exp(-apart * apart / spread_sq),
            0.0,
        )
        filt[n] = taps[HALO : HALO + rows]
        own = lax.broadcasted_iota(jnp.int32, (rows, reach), 0).astype(F32)
        middle = lax.broadcasted_iota(jnp.int32, (rows, reach), 1).astype(F32) - HALO
        away = middle - own
        first = jnp.where(jnp.abs(away) <= HALO, 0.5 * jnp.exp(-away * away / spread_sq), 0.0)
        filt2[n] = jnp.dot(
            first, taps, precision=lax.Precision.HIGHEST, preferred_element_type=F32
        )
        band = lat + offset(n)
        inside = jnp.where((band >= 0) & (band < n_lat), 1.0, 0.0)
        target[pl.ds(n, 1), :] = meta[n, 1:2, :]
        scale[pl.ds(n, 1), :] = meta[n, 2:3, :]
        live[pl.ds(n, 1), :] = meta[n, 3:4, :] * inside

    pl.semaphore_wait(barrier, n_mem + n_lat - 2)

    @pl.loop(1, NEAR)
    def _(n):
        meta_copy(n).start()

    @pl.loop(1, 3)
    def _(n):
        value_copy(n).start()

    @pl.loop(0, NEAR)
    def _(n):
        @pl.when(n > 0)
        def _():
            meta_copy(n).wait_recv()

        @pl.when(n == 1)
        def _():
            value_copy(3).start()
            value_copy(4).start()

        prepare(n)

    image_acc[...] = jnp.zeros_like(image_acc)
    control_ref[...] = jnp.zeros_like(control_ref)

    def scattered(filter_ref, bands, first):
        acc[...] = jnp.zeros_like(acc)

        @pl.loop(0, bands)
        def _(n):
            @pl.when(first & (n > 0))
            def _():
                value_copy(n).wait_recv()

            @pl.when(first)
            def _():
                values = jnp.broadcast_to(bvals[n][:, None, :], (members, rows, slots))
                spread[n] = values.reshape(flat, slots).astype(BF16)

            factor = filter_ref[n] * q_now[pl.ds(n, 1), :]
            value = spread[n].astype(F32).reshape(members, rows, slots) * factor[None]
            high, low = halves(value.reshape(flat, slots))
            acc[...] += lax.dot_general(
                jnp.concatenate([high, low], axis=0),
                onehot[n],
                (((1,), (1,)), ((), ())),
                preferred_element_type=F32,
            )

        return acc[:flat] + acc[flat:]

    def filtered(value, which):
        high, low = halves(value)
        both = jnp.concatenate([high, low], axis=0)
        vext[:, PAD : PAD + cols] = both
        vext[:, :PAD] = both[:, cols - PAD :]
        vext[:, PAD + cols :] = both[:, :PAD]
        blocks = []
        for j in range(cols // BLOCK):
            window = vext[:, j * BLOCK : j * BLOCK + BLOCK + 2 * PAD]
            product = dot(window, win_ref[2 * which])
            blocks.append(
                product[:flat] + product[flat:] + dot(window[:flat], win_ref[2 * which + 1])
            )
        return blocks

    def send_image(k):
        @pl.loop(1, n_mem)
        def _(r):
            to = lax.rem(mem + r, n_mem)
            width = inc_ref.shape[1]
            part = pl.ds(pl.multiple_of(to * width, 128), width)
            remote(
                image.at[k, :, part], irecv.at[k, r - 1], i_send.at[k], i_recv.at[k], mem_peer(r)
            ).start()

    @pl.loop(0, ITERS)
    def _(t):
        last = t == ITERS - 1
        bounded = jnp.tanh((target[...] - observed[...]) / scale[...])
        q_now[...] = live[...] * (scale[...] * bounded) - summed[...]
        weight[...] = (live[...] * (1.0 - bounded * bounded))[0:1]

        for j, block in enumerate(filtered(scattered(filt2, NEAR, t == 0), 1)):
            high, low = halves(block)
            vwide[:, j * BLOCK : (j + 1) * BLOCK] = jnp.concatenate([high, low], axis=0)
        vwide[:, cols:] = vwide[:, :PAD]

        seen = dot(vwide[:, :cols], onehot[0])
        hits_part = c * jnp.sum(
            chosen[...].astype(F32) * (seen[:flat] + seen[flat:]), axis=0, keepdims=True
        )
        hsend[t] = hits_part

        @pl.loop(1, n_mem)
        def _(r):
            remote(
                hsend.at[t], hrecv.at[t, r - 1], h_send.at[t], h_recv.at[t], mem_peer(r)
            ).start()

        at_t = jnp.where(last, 1, 0)
        for j in range(fine_cols // 256):
            wide = dot(vwide[:, 128 * j : 128 * j + 256], widen_ref[...])
            wide = (wide[:flat] + wide[flat:]).reshape(members, rows, 256)
            here = slice(256 * j, 256 * (j + 1))
            for e in range(2):
                pert = picked[e * flat : (e + 1) * flat, here].astype(F32)
                total = c * jnp.sum(pert.reshape(members, rows, 256) * wide, axis=0)
                image[at_t, e * rows : (e + 1) * rows, here] = total

        @pl.when(last)
        def _():
            send_image(1)

        wait_all(hrecv.at[t], h_recv.at[t])
        hits = hits_part + jnp.sum(hrecv[t], axis=0)
        q_own = q_now[0:1, :]
        gg_part = q_own * hits
        cc_part = weight[...] * hits * hits
        width = 128
        ssend[t, :, :width] = sum(
            gg_part[:, i : i + width] for i in range(0, slots, width)
        )
        ssend[t, :, width:] = sum(
            cc_part[:, i : i + width] for i in range(0, slots, width)
        )

        @pl.loop(1, n_lat)
        def _(r):
            remote(
                ssend.at[t], srecv.at[t, r - 1], s_send.at[t], s_recv.at[t], lat_peer(r)
            ).start()

        @pl.when(jnp.logical_not(last))
        def _():
            hnear[t, 0] = hits

        def near_hits(n):
            return remote(
                hnear.at[t, 0],
                hnear.at[t, n],
                n_send.at[t, n - 1],
                n_recv.at[t, n - 1],
                near_peer(n),
            )

        @pl.when(jnp.logical_not(last))
        def _():
            @pl.loop(1, NEAR)
            def _(n):
                near_hits(n).start()

        for j, block in enumerate(filtered(scattered(filt, 3, t < 0), 0)):
            along[:, j * BLOCK : (j + 1) * BLOCK] = block

        wait_all(srecv.at[t], s_recv.at[t])
        sums = ssend[t] + jnp.sum(srecv[t], axis=0)
        gg = jnp.maximum(jnp.sum(sums[:, :width], axis=1, keepdims=True), 0.0)
        cc = jnp.sum(sums[:, width:], axis=1, keepdims=True)
        step = gg / (gg + cc + 1e-6)

        control_ref[...] += step[None] * along[...].reshape(members, rows, cols)
        summed[...] += step * q_now[...]
        observed[0:1, :] += step * hits

        @pl.when(jnp.logical_not(last))
        def _():
            @pl.loop(1, NEAR)
            def _(n):
                near_hits(n).wait_recv()
                observed[pl.ds(n, 1), :] += step * hnear[t, n]

            image_acc[...] += step * image[0]

        @pl.when(t == ITERS - 2)
        def _():
            image[0] = image_acc[...]
            send_image(0)

        @pl.when(last)
        def _():
            width = inc_ref.shape[1]
            part = pl.ds(pl.multiple_of(mem * width, 128), width)
            wait_all(irecv.at[0], i_recv.at[0])
            wait_all(irecv.at[1], i_recv.at[1])
            before = image[0, :, part] + jnp.sum(irecv[0], axis=0)
            now = image[1, :, part] + jnp.sum(irecv[1], axis=0)
            total = before + step * now
            for e in range(2):
                inc_ref[pl.ds(e, rows, 2), :] = total[e * rows : (e + 1) * rows]

    @pl.loop(1, NEAR)
    def _(n):
        meta_copy(n).wait_send()
        value_copy(n).wait_send()

    @pl.loop(0, ITERS)
    def _(t):
        wait_all(hrecv.at[t], h_send.at[t])
        wait_all(srecv.at[t], s_send.at[t])

        @pl.when(t < ITERS - 1)
        def _():
            @pl.loop(1, NEAR)
            def _(n):
                wait_all(hnear.at[t, n], n_send.at[t, n - 1])

    wait_all(irecv.at[0], i_send.at[0])
    wait_all(irecv.at[1], i_send.at[1])


def on_device(n_mem, n_lat, windows, pert, cells, count, innov, scale):
    members, fine_rows, fine_cols = pert.shape
    rows, cols = fine_rows // 2, fine_cols // 2
    slots = cells.shape[1]
    flat = members * rows
    width = fine_cols // n_mem
    vmem = pl.BlockSpec(memory_space=pltpu.VMEM)
    scratch = [
        pltpu.VMEM((NEAR, 4, slots), F32),
        pltpu.VMEM((NEAR, members, slots), F32),
        pltpu.VMEM((NEAR, flat, slots), BF16),
        pltpu.VMEM((flat, slots), BF16),
        pltpu.VMEM((2 * flat, fine_cols), BF16),
        pltpu.VMEM((NEAR, cols, slots), BF16),
        pltpu.VMEM((NEAR, rows, slots), F32),
        pltpu.VMEM((NEAR, rows, slots), F32),
        pltpu.VMEM((8, slots), F32),
        pltpu.VMEM((8, slots), F32),
        pltpu.VMEM((8, slots), F32),
        pltpu.VMEM((8, slots), F32),
        pltpu.VMEM((8, slots), F32),
        pltpu.VMEM((8, slots), F32),
        pltpu.VMEM((1, slots), F32),
        pltpu.VMEM((2 * flat, cols), F32),
        pltpu.VMEM((2 * flat, cols + 2 * PAD), BF16),
        pltpu.VMEM((2 * flat, cols + PAD), BF16),
        pltpu.VMEM((flat, cols), F32),
        pltpu.VMEM((2, fine_rows, fine_cols), F32),
        pltpu.VMEM((fine_rows, fine_cols), F32),
        pltpu.VMEM((ITERS, 1, slots), F32),
        pltpu.VMEM((ITERS, n_mem - 1, 1, slots), F32),
        pltpu.VMEM((ITERS - 1, NEAR, 1, slots), F32),
        pltpu.VMEM((ITERS, 1, 256), F32),
        pltpu.VMEM((ITERS, n_lat - 1, 1, 256), F32),
        pltpu.VMEM((2, n_mem - 1, fine_rows, width), F32),
    ]
    scratch += [pltpu.SemaphoreType.DMA((NEAR - 1,))] * 4
    scratch += [pltpu.SemaphoreType.DMA((ITERS,))] * 2
    scratch += [pltpu.SemaphoreType.DMA((ITERS - 1, NEAR - 1))] * 2
    scratch += [pltpu.SemaphoreType.DMA((ITERS,))] * 2
    scratch += [pltpu.SemaphoreType.DMA((2,))] * 2
    control, increment = pl.pallas_call(
        functools.partial(body, n_mem, n_lat),
        out_shape=(
            jax.ShapeDtypeStruct((members, rows, cols), F32),
            jax.ShapeDtypeStruct((fine_rows, width), F32),
        ),
        in_specs=[vmem, pl.BlockSpec(memory_space=pltpu.SMEM)] + [vmem] * 6,
        out_specs=(vmem, vmem),
        scratch_shapes=scratch,
        compiler_params=pltpu.CompilerParams(
            collective_id=0, has_side_effects=True, vmem_limit_bytes=60 * 2**20
        ),
    )(
        cells,
        count,
        innov,
        scale,
        pert,
        jnp.asarray(split_rows_matrix(members, fine_rows)),
        jnp.asarray(windows),
        jnp.asarray(widen_matrix()),
    )
    return control, increment


def solution(mesh):
    n_mem, n_lat = mesh.shape["mem"], mesh.shape["lat"]

    def run(pert, cells, count, innov, scale):
        windows = window_matrices(pert.shape[2] // 2)
        return on_device(n_mem, n_lat, windows, pert, cells, count, innov, scale)

    return jax.shard_map(
        run,
        mesh=mesh,
        in_specs=(P("mem", "lat", None), P("lat", None), P("lat"), P("lat", None), P("lat", None)),
        out_specs=(P("mem", "lat", None), P("lat", "mem")),
        check_vma=False,
    )
```

```python
import functools

import jax
import jax.numpy as jnp
import ml_dtypes
import numpy as np
from jax import lax
from jax.experimental import pallas as pl
from jax.experimental.pallas import tpu as pltpu
from jax.sharding import PartitionSpec as P

HALO = 8
LSIG = 3
ITERS = 3
NEAR = 5
BLOCK = 256
STRIDE = 255
PAD = 128
F32 = jnp.float32
BF16 = jnp.bfloat16
MESH = pl.DeviceIdType.MESH


def window_matrices(coarse_cols):
    columns = np.arange(coarse_cols)
    distance = np.minimum(columns, coarse_cols - columns).astype(np.float32)
    first = np.exp(-distance * distance / np.float32(2.0 * LSIG * LSIG)).astype(np.float64)
    circulant = first[np.abs(columns[:, None] - columns[None, :])]
    squared = first @ circulant
    apart = np.arange(BLOCK + 2 * PAD)[:, None] - PAD - np.arange(BLOCK)[None, :]
    parts = []
    for row in (first, squared):
        inside = np.abs(apart) < min(PAD, coarse_cols // 2)
        window = np.where(inside, row[np.abs(apart) % coarse_cols], 0.0).astype(np.float32)
        high = window.astype(ml_dtypes.bfloat16)
        parts += [high, (window - high.astype(np.float32)).astype(ml_dtypes.bfloat16)]
    return np.stack(parts)


def widen_matrix():
    fine = np.arange(256) * 0.5
    coarse = np.arange(256)
    return np.maximum(0.0, 1.0 - np.abs(coarse[:, None] - fine[None, :])).astype(
        ml_dtypes.bfloat16
    )


def split_rows_matrix(members, rows):
    matrix = np.zeros((members * rows, members * rows), ml_dtypes.bfloat16)
    for member in range(members):
        for row in range(rows):
            to = (row % 2) * members * (rows // 2) + member * (rows // 2) + row // 2
            matrix[to, member * rows + row] = 1.0
    return matrix


def halves(value):
    high = value.astype(BF16)
    return high, (value - high.astype(F32)).astype(BF16)


def dot(a, b):
    return jnp.dot(a, b, preferred_element_type=F32)


def body(
    n_mem,
    n_lat,
    cells_ref,
    count_ref,
    innov_ref,
    scale_ref,
    pert_ref,
    sel_ref,
    win_ref,
    widen_ref,
    control_ref,
    inc_ref,
    meta,
    bvals,
    spread,
    chosen,
    picked,
    onehot,
    tile,
    columns,
    last_chunk,
    keys,
    rank,
    unsorted,
    left_even,
    left_odd,
    running,
    whole,
    filt,
    filt2,
    target,
    scale,
    live,
    observed,
    summed,
    q_now,
    weight,
    acc,
    vext,
    vwide,
    along,
    image,
    image_acc,
    hsend,
    hrecv,
    hnear,
    ssend,
    srecv,
    irecv,
    meta_send,
    meta_recv,
    b_send,
    b_recv,
    h_send,
    h_recv,
    n_send,
    n_recv,
    s_send,
    s_recv,
    i_send,
    i_recv,
):
    members, fine_rows, fine_cols = pert_ref.shape
    rows, cols = fine_rows // 2, fine_cols // 2
    slots = cells_ref.shape[1]
    flat = members * rows
    c = float((members * n_mem - 1) ** -0.5)
    mem = lax.axis_index("mem")
    lat = lax.axis_index("lat")
    barrier = pltpu.get_barrier_semaphore()

    def mem_peer(r):
        return {"mem": lax.rem(mem + r, n_mem)}

    def lat_peer(r):
        return {"lat": lax.rem(lat + r, n_lat)}

    def offset(n):
        return ((n + 1) // 2) * (1 - 2 * (n % 2))

    def remote(src, dst, send, recv, device):
        return pltpu.make_async_remote_copy(
            src_ref=src,
            dst_ref=dst,
            send_sem=send,
            recv_sem=recv,
            device_id=device,
            device_id_type=MESH,
        )

    def wait_all(ref, sem):
        pltpu.make_async_copy(ref, ref, sem).wait()

    @pl.loop(1, n_mem)
    def _(r):
        pl.semaphore_signal(barrier, inc=1, device_id=mem_peer(r), device_id_type=MESH)

    @pl.loop(1, n_lat)
    def _(r):
        pl.semaphore_signal(barrier, inc=1, device_id=lat_peer(r), device_id_type=MESH)

    cells = cells_ref[...]
    slot_id = lax.broadcasted_iota(jnp.int32, (1, slots), 1)
    chunks = slots // BLOCK
    blocks = -(-cols // STRIDE)
    tiles = chunks + blocks - 1

    column_id = cells & (fine_cols - 1)
    key = (column_id * slots + slot_id).astype(F32)
    keys[...] = jnp.broadcast_to(key, (128, slots)).T
    rank[...] = key

    @pl.loop(0, slots // 128)
    def _(j):
        at = pl.ds(pl.multiple_of(j * 128, 128), 128)
        below = jnp.where(keys[...] < rank[:, at], 1.0, 0.0)
        rank[:, at] = jnp.sum(below, axis=0, keepdims=True)

    def thirds(value):
        high = value.astype(BF16).astype(F32)
        middle = (value - high).astype(BF16).astype(F32)
        return [high, middle, value - high - middle]

    given = jnp.concatenate(
        [(cells >> 8).astype(F32), (cells & 255).astype(F32)]
        + thirds(innov_ref[...])
        + thirds(scale_ref[...])
        + [jnp.where(slot_id < count_ref[0], 1.0, 0.0)]
        + [jnp.zeros((7, slots), F32)],
        axis=0,
    )
    unsorted[...] = given.astype(BF16)

    @pl.loop(0, chunks)
    def _(j):
        start = pl.multiple_of(j * BLOCK, BLOCK)
        to = (lax.broadcasted_iota(jnp.int32, (BLOCK, slots), 0) + start).astype(F32)
        move = jnp.where(to == rank[...], 1.0, 0.0).astype(BF16)
        moved = lax.dot_general(
            unsorted[...], move, (((1,), (1,)), ((), ())), preferred_element_type=F32
        )
        at = pl.ds(start, BLOCK)
        meta[0, 0:1, at] = moved[0:1] * 256.0 + moved[1:2]
        meta[0, 1:2, at] = moved[2:3] + moved[3:4] + moved[4:5]
        meta[0, 2:3, at] = moved[5:6] + moved[6:7] + moved[7:8]
        meta[0, 3:4, at] = moved[8:9]

    def place_of(n, at):
        cell = meta[n, 0:1, at]
        fine_row = jnp.floor(cell * (1.0 / fine_cols))
        return fine_row, cell - fine_row * float(fine_cols)

    def near_peer(n):
        return {"lat": lax.rem(lat - offset(n) + n_lat, n_lat)}

    def meta_copy(n):
        return remote(
            meta.at[0], meta.at[n], meta_send.at[n - 1], meta_recv.at[n - 1], near_peer(n)
        )

    def value_copy(n):
        return remote(
            bvals.at[0], bvals.at[n], b_send.at[n - 1], b_recv.at[n - 1], near_peer(n)
        )

    @pl.loop(0, fine_cols // BLOCK)
    def _(j):
        at = pl.ds(pl.multiple_of(j * BLOCK, BLOCK), BLOCK)
        picked[:, at] = dot(
            sel_ref[...], pert_ref[:, :, at].reshape(members * fine_rows, BLOCK)
        ).astype(BF16)

    @pl.loop(0, slots // BLOCK)
    def _(j):
        at = pl.ds(pl.multiple_of(j * BLOCK, BLOCK), BLOCK)
        fine_row, column = place_of(0, at)
        coarse_row = jnp.floor(fine_row * 0.5)
        place = lax.broadcasted_iota(jnp.int32, (fine_cols, BLOCK), 0).astype(F32)
        hit = jnp.where(place == column, 1.0, 0.0).astype(BF16)
        both = dot(picked[...], hit)
        odd = fine_row - 2.0 * coarse_row
        value = jnp.where(odd > 0.5, both[flat:], both[:flat])
        own = lax.broadcasted_iota(jnp.int32, (rows, BLOCK), 0).astype(F32) == coarse_row
        value = jnp.where(own[None], value.reshape(members, rows, BLOCK), 0.0)
        chosen[:, at] = value.reshape(flat, BLOCK).astype(BF16)
        bvals[0, :, at] = jnp.sum(value, axis=1)

    target[...] = jnp.zeros_like(target)
    scale[...] = jnp.ones_like(scale)
    live[...] = jnp.zeros_like(live)
    observed[...] = jnp.zeros_like(observed)
    summed[...] = jnp.zeros_like(summed)

    def block_of(n, p):
        block = jnp.int32(0)
        for j in range(blocks - 1):
            block += jnp.where(last_chunk[n, j] + j < p, 1, 0).astype(jnp.int32)
        return jnp.maximum(block, p - (chunks - 1))

    def prepare_own():
        x = place_of(0, slice(None))[1] * 0.5
        step = 128
        place16 = lax.broadcasted_iota(jnp.int32, (step, slots), 0).astype(F32).astype(BF16)

        @pl.loop(0, cols // step)
        def _(j):
            start = pl.multiple_of(j * step, step)
            near = jnp.clip(x - start.astype(F32), -2.0, step + 1.0).astype(BF16)
            apart = jnp.abs(near - place16)
            onehot[pl.ds(start, step), :] = jnp.maximum(BF16(1.0) - apart, BF16(0.0))

        place = lax.broadcasted_iota(jnp.int32, (16, slots), 0).astype(F32)
        hat = jnp.maximum(
            jnp.maximum(1.0 - jnp.abs(x - place), 1.0 - jnp.abs(x - (place + float(cols)))), 0.0
        )
        onehot[0:16, :] = hat.astype(BF16)

    def prepare(n):
        fine_row, column = place_of(n, slice(None))
        x = column * 0.5
        for j in range(chunks):
            columns[j] = x[:, j * BLOCK : (j + 1) * BLOCK]
        for j in range(blocks - 1):
            count = jnp.sum(jnp.where(x < float(STRIDE * (j + 1)), 1.0, 0.0)).astype(jnp.int32)
            last_chunk[n, j] = jnp.clip(((count + BLOCK - 1) >> 8) - 1, 0, chunks - 1)
        for p in range(tiles):
            block = block_of(n, p)
            local = columns[p - block] - (block * STRIDE).astype(F32)
            local = jnp.where((local >= 0.0) & (local < float(STRIDE)), local, -9.0)
            place = lax.broadcasted_iota(jnp.int32, (BLOCK, BLOCK), 0).astype(F32)
            tile[n, p] = jnp.maximum(1.0 - jnp.abs(local - place), 0.0).astype(BF16)

        reach = rows + 2 * HALO
        between = lax.broadcasted_iota(jnp.int32, (reach, slots), 0) - HALO
        global_row = between + lat * rows
        shift = jnp.asarray(offset(n) * rows, jnp.int32).astype(F32)
        apart = between.astype(F32) - (jnp.floor(fine_row * 0.5) + shift)
        spread_sq = 2.0 * (HALO / 2.0) ** 2
        taps = jnp.where(
            (jnp.abs(apart) <= HALO) & (global_row >= 0) & (global_row < n_lat * rows),
            (0.5 * c) * jnp.exp(-apart * apart / spread_sq),
            0.0,
        )
        filt[n] = taps[HALO : HALO + rows]
        own = lax.broadcasted_iota(jnp.int32, (rows, reach), 0).astype(F32)
        middle = lax.broadcasted_iota(jnp.int32, (rows, reach), 1).astype(F32) - HALO
        away = middle - own
        first = jnp.where(jnp.abs(away) <= HALO, 0.5 * jnp.exp(-away * away / spread_sq), 0.0)
        filt2[n] = jnp.dot(
            first, taps, precision=lax.Precision.HIGHEST, preferred_element_type=F32
        )
        band = lat + offset(n)
        inside = jnp.where((band >= 0) & (band < n_lat), 1.0, 0.0)
        target[pl.ds(n, 1), :] = meta[n, 1:2, :]
        scale[pl.ds(n, 1), :] = meta[n, 2:3, :]
        live[pl.ds(n, 1), :] = meta[n, 3:4, :] * inside

    prepare_own()
    pl.semaphore_wait(barrier, n_mem + n_lat - 2)

    @pl.loop(1, NEAR)
    def _(n):
        meta_copy(n).start()

    @pl.loop(1, 3)
    def _(n):
        value_copy(n).start()

    @pl.loop(0, NEAR)
    def _(n):
        @pl.when(n > 0)
        def _():
            meta_copy(n).wait_recv()

        @pl.when(n == 1)
        def _():
            value_copy(3).start()
            value_copy(4).start()

        prepare(n)

    image_acc[...] = jnp.zeros_like(image_acc)
    control_ref[...] = jnp.zeros_like(control_ref)

    lefts = (left_even, left_odd)

    def scattered(filter_ref, bands, first):
        acc[...] = jnp.zeros_like(acc)

        def values_of(n):
            @pl.when(first)
            def _():
                if n > 0:
                    value_copy(n).wait_recv()
                values = jnp.broadcast_to(bvals[n][:, None, :], (members, rows, slots))
                spread[n] = values.reshape(flat, slots).astype(BF16)

        def weigh(n):
            left = lefts[n % 2]
            factor = filter_ref[n] * q_now[n : n + 1, :]
            for j in range(chunks):
                here = slice(j * BLOCK, (j + 1) * BLOCK)
                value = spread[n, :, here].astype(F32).reshape(members, rows, BLOCK)
                high, low = halves((value * factor[None, :, here]).reshape(flat, BLOCK))
                left[j, :flat] = high
                left[j, flat:] = low

        def multiply(n):
            left = lefts[n % 2]
            before = None
            for p in range(tiles):
                block = block_of(n, p)
                product = lax.dot_general(
                    left[p - block],
                    tile[n, p],
                    (((1,), (1,)), ((), ())),
                    preferred_element_type=F32,
                )
                total = product[:flat] + product[flat:]
                if p > 0:
                    total += jnp.where(block == before, 1.0, 0.0) * running[p - 1]
                running[p] = total
                before = block
            for j in range(blocks):
                end = last_chunk[n, j] + j if j < blocks - 1 else tiles - 1
                acc[j] += running[end]

        values_of(0)
        weigh(0)
        for n in range(bands):
            if n + 1 < bands:
                values_of(n + 1)
                weigh(n + 1)
            multiply(n)

        whole[...] = jnp.zeros_like(whole)
        whole[:, :BLOCK] = acc[0]
        for j in range(1, blocks):
            wide = jnp.concatenate([acc[j], jnp.zeros((flat, 128), F32)], axis=1)
            start = BLOCK * j - 128
            whole[:, start : start + BLOCK + 128] += pltpu.roll(wide, 128 - j, 1)
        whole[:, :128] += whole[:, cols : cols + 128]
        return whole[:, :cols]

    def filtered(value, which):
        high, low = halves(value)
        both = jnp.concatenate([high, low], axis=0)
        vext[:, PAD : PAD + cols] = both
        vext[:, :PAD] = both[:, cols - PAD :]
        vext[:, PAD + cols :] = both[:, :PAD]
        blocks = []
        for j in range(cols // BLOCK):
            window = vext[:, j * BLOCK : j * BLOCK + BLOCK + 2 * PAD]
            product = dot(window, win_ref[2 * which])
            blocks.append(
                product[:flat] + product[flat:] + dot(window[:flat], win_ref[2 * which + 1])
            )
        return blocks

    def send_image(k):
        @pl.loop(1, n_mem)
        def _(r):
            to = lax.rem(mem + r, n_mem)
            width = inc_ref.shape[1]
            part = pl.ds(pl.multiple_of(to * width, 128), width)
            remote(
                image.at[k, :, part], irecv.at[k, r - 1], i_send.at[k], i_recv.at[k], mem_peer(r)
            ).start()

    @pl.loop(0, ITERS)
    def _(t):
        last = t == ITERS - 1
        bounded = jnp.tanh((target[...] - observed[...]) / scale[...])
        q_now[...] = live[...] * (scale[...] * bounded) - summed[...]
        weight[...] = (live[...] * (1.0 - bounded * bounded))[0:1]

        for j, block in enumerate(filtered(scattered(filt2, NEAR, t == 0), 1)):
            high, low = halves(block)
            vwide[:, j * BLOCK : (j + 1) * BLOCK] = jnp.concatenate([high, low], axis=0)
        vwide[:, cols:] = vwide[:, :PAD]

        seen = dot(vwide[:, :cols], onehot[...])
        hits_part = c * jnp.sum(
            chosen[...].astype(F32) * (seen[:flat] + seen[flat:]), axis=0, keepdims=True
        )
        hsend[t] = hits_part

        @pl.loop(1, n_mem)
        def _(r):
            remote(
                hsend.at[t], hrecv.at[t, r - 1], h_send.at[t], h_recv.at[t], mem_peer(r)
            ).start()

        at_t = jnp.where(last, 1, 0)
        for j in range(fine_cols // 256):
            wide = dot(vwide[:, 128 * j : 128 * j + 256], widen_ref[...])
            wide = (wide[:flat] + wide[flat:]).reshape(members, rows, 256)
            here = slice(256 * j, 256 * (j + 1))
            for e in range(2):
                pert = picked[e * flat : (e + 1) * flat, here].astype(F32)
                total = c * jnp.sum(pert.reshape(members, rows, 256) * wide, axis=0)
                image[at_t, e * rows : (e + 1) * rows, here] = total

        @pl.when(last)
        def _():
            send_image(1)

        wait_all(hrecv.at[t], h_recv.at[t])
        hits = hits_part + jnp.sum(hrecv[t], axis=0)
        q_own = q_now[0:1, :]
        gg_part = q_own * hits
        cc_part = weight[...] * hits * hits
        width = 128
        ssend[t, :, :width] = sum(
            gg_part[:, i : i + width] for i in range(0, slots, width)
        )
        ssend[t, :, width:] = sum(
            cc_part[:, i : i + width] for i in range(0, slots, width)
        )

        @pl.loop(1, n_lat)
        def _(r):
            remote(
                ssend.at[t], srecv.at[t, r - 1], s_send.at[t], s_recv.at[t], lat_peer(r)
            ).start()

        @pl.when(jnp.logical_not(last))
        def _():
            hnear[t, 0] = hits

        def near_hits(n):
            return remote(
                hnear.at[t, 0],
                hnear.at[t, n],
                n_send.at[t, n - 1],
                n_recv.at[t, n - 1],
                near_peer(n),
            )

        @pl.when(jnp.logical_not(last))
        def _():
            @pl.loop(1, NEAR)
            def _(n):
                near_hits(n).start()

        for j, block in enumerate(filtered(scattered(filt, 3, t < 0), 0)):
            along[:, j * BLOCK : (j + 1) * BLOCK] = block

        wait_all(srecv.at[t], s_recv.at[t])
        sums = ssend[t] + jnp.sum(srecv[t], axis=0)
        gg = jnp.maximum(jnp.sum(sums[:, :width], axis=1, keepdims=True), 0.0)
        cc = jnp.sum(sums[:, width:], axis=1, keepdims=True)
        step = gg / (gg + cc + 1e-6)

        control_ref[...] += step[None] * along[...].reshape(members, rows, cols)
        summed[...] += step * q_now[...]
        observed[0:1, :] += step * hits

        @pl.when(jnp.logical_not(last))
        def _():
            @pl.loop(1, NEAR)
            def _(n):
                near_hits(n).wait_recv()
                observed[pl.ds(n, 1), :] += step * hnear[t, n]

            image_acc[...] += step * image[0]

        @pl.when(t == ITERS - 2)
        def _():
            image[0] = image_acc[...]
            send_image(0)

        @pl.when(last)
        def _():
            width = inc_ref.shape[1]
            part = pl.ds(pl.multiple_of(mem * width, 128), width)
            wait_all(irecv.at[0], i_recv.at[0])
            wait_all(irecv.at[1], i_recv.at[1])
            before = image[0, :, part] + jnp.sum(irecv[0], axis=0)
            now = image[1, :, part] + jnp.sum(irecv[1], axis=0)
            total = before + step * now
            for e in range(2):
                inc_ref[pl.ds(e, rows, 2), :] = total[e * rows : (e + 1) * rows]

    @pl.loop(1, NEAR)
    def _(n):
        meta_copy(n).wait_send()
        value_copy(n).wait_send()

    @pl.loop(0, ITERS)
    def _(t):
        wait_all(hrecv.at[t], h_send.at[t])
        wait_all(srecv.at[t], s_send.at[t])

        @pl.when(t < ITERS - 1)
        def _():
            @pl.loop(1, NEAR)
            def _(n):
                wait_all(hnear.at[t, n], n_send.at[t, n - 1])

    wait_all(irecv.at[0], i_send.at[0])
    wait_all(irecv.at[1], i_send.at[1])


def on_device(n_mem, n_lat, windows, pert, cells, count, innov, scale):
    members, fine_rows, fine_cols = pert.shape
    rows, cols = fine_rows // 2, fine_cols // 2
    slots = cells.shape[1]
    flat = members * rows
    width = fine_cols // n_mem
    chunks = slots // BLOCK
    blocks = -(-cols // STRIDE)
    tiles = chunks + blocks - 1
    vmem = pl.BlockSpec(memory_space=pltpu.VMEM)
    scratch = [
        pltpu.VMEM((NEAR, 4, slots), F32),
        pltpu.VMEM((NEAR, members, slots), F32),
        pltpu.VMEM((NEAR, flat, slots), BF16),
        pltpu.VMEM((flat, slots), BF16),
        pltpu.VMEM((2 * flat, fine_cols), BF16),
        pltpu.VMEM((cols, slots), BF16),
        pltpu.VMEM((NEAR, tiles, BLOCK, BLOCK), BF16),
        pltpu.VMEM((chunks, 1, BLOCK), F32),
        pltpu.SMEM((NEAR, 8), jnp.int32),
        pltpu.VMEM((slots, 128), F32),
        pltpu.VMEM((1, slots), F32),
        pltpu.VMEM((16, slots), BF16),
        pltpu.VMEM((chunks, 2 * flat, BLOCK), BF16),
        pltpu.VMEM((chunks, 2 * flat, BLOCK), BF16),
        pltpu.VMEM((tiles, flat, BLOCK), F32),
        pltpu.VMEM((flat, cols + 256), F32),
        pltpu.VMEM((NEAR, rows, slots), F32),
        pltpu.VMEM((NEAR, rows, slots), F32),
        pltpu.VMEM((8, slots), F32),
        pltpu.VMEM((8, slots), F32),
        pltpu.VMEM((8, slots), F32),
        pltpu.VMEM((8, slots), F32),
        pltpu.VMEM((8, slots), F32),
        pltpu.VMEM((8, slots), F32),
        pltpu.VMEM((1, slots), F32),
        pltpu.VMEM((blocks, flat, BLOCK), F32),
        pltpu.VMEM((2 * flat, cols + 2 * PAD), BF16),
        pltpu.VMEM((2 * flat, cols + PAD), BF16),
        pltpu.VMEM((flat, cols), F32),
        pltpu.VMEM((2, fine_rows, fine_cols), F32),
        pltpu.VMEM((fine_rows, fine_cols), F32),
        pltpu.VMEM((ITERS, 1, slots), F32),
        pltpu.VMEM((ITERS, n_mem - 1, 1, slots), F32),
        pltpu.VMEM((ITERS - 1, NEAR, 1, slots), F32),
        pltpu.VMEM((ITERS, 1, 256), F32),
        pltpu.VMEM((ITERS, n_lat - 1, 1, 256), F32),
        pltpu.VMEM((2, n_mem - 1, fine_rows, width), F32),
    ]
    scratch += [pltpu.SemaphoreType.DMA((NEAR - 1,))] * 4
    scratch += [pltpu.SemaphoreType.DMA((ITERS,))] * 2
    scratch += [pltpu.SemaphoreType.DMA((ITERS - 1, NEAR - 1))] * 2
    scratch += [pltpu.SemaphoreType.DMA((ITERS,))] * 2
    scratch += [pltpu.SemaphoreType.DMA((2,))] * 2
    control, increment = pl.pallas_call(
        functools.partial(body, n_mem, n_lat),
        out_shape=(
            jax.ShapeDtypeStruct((members, rows, cols), F32),
            jax.ShapeDtypeStruct((fine_rows, width), F32),
        ),
        in_specs=[vmem, pl.BlockSpec(memory_space=pltpu.SMEM)] + [vmem] * 6,
        out_specs=(vmem, vmem),
        scratch_shapes=scratch,
        compiler_params=pltpu.CompilerParams(
            collective_id=0, has_side_effects=True, vmem_limit_bytes=60 * 2**20
        ),
    )(
        cells,
        count,
        innov,
        scale,
        pert,
        jnp.asarray(split_rows_matrix(members, fine_rows)),
        jnp.asarray(windows),
        jnp.asarray(widen_matrix()),
    )
    return control, increment


def solution(mesh):
    n_mem, n_lat = mesh.shape["mem"], mesh.shape["lat"]

    def run(pert, cells, count, innov, scale):
        windows = window_matrices(pert.shape[2] // 2)
        return on_device(n_mem, n_lat, windows, pert, cells, count, innov, scale)

    return jax.shard_map(
        run,
        mesh=mesh,
        in_specs=(P("mem", "lat", None), P("lat", None), P("lat"), P("lat", None), P("lat", None)),
        out_specs=(P("mem", "lat", None), P("lat", "mem")),
        check_vma=False,
    )
```

```python
import functools

import jax
import jax.numpy as jnp
import ml_dtypes
import numpy as np
from jax import lax
from jax.experimental import pallas as pl
from jax.experimental.pallas import tpu as pltpu
from jax.sharding import PartitionSpec as P

HALO = 8
LSIG = 3
ITERS = 3
NEAR = 5
BLOCK = 256
PAD = 128
F32 = jnp.float32
BF16 = jnp.bfloat16
F8 = jnp.float8_e4m3fn
ROOM = 32.0
MESH = pl.DeviceIdType.MESH


def window_matrices(coarse_cols):
    columns = np.arange(coarse_cols)
    distance = np.minimum(columns, coarse_cols - columns).astype(np.float32)
    first = np.exp(-distance * distance / np.float32(2.0 * LSIG * LSIG)).astype(np.float64)
    circulant = first[np.abs(columns[:, None] - columns[None, :])]
    squared = first @ circulant
    apart = np.arange(BLOCK + 2 * PAD)[:, None] - PAD - np.arange(BLOCK)[None, :]
    parts = []
    for row in (first, squared):
        inside = np.abs(apart) < min(PAD, coarse_cols // 2)
        window = np.where(inside, row[np.abs(apart) % coarse_cols], 0.0).astype(np.float32)
        high = window.astype(ml_dtypes.bfloat16)
        parts += [high, (window - high.astype(np.float32)).astype(ml_dtypes.bfloat16)]
    return np.stack(parts)


def widen_matrix():
    fine = np.arange(256) * 0.5
    coarse = np.arange(256)
    return np.maximum(0.0, 1.0 - np.abs(coarse[:, None] - fine[None, :])).astype(
        ml_dtypes.bfloat16
    )


def split_rows_matrix(members, rows):
    matrix = np.zeros((members * rows, members * rows), ml_dtypes.bfloat16)
    for member in range(members):
        for row in range(rows):
            to = (row % 2) * members * (rows // 2) + member * (rows // 2) + row // 2
            matrix[to, member * rows + row] = 1.0
    return matrix


def halves(value):
    high = value.astype(BF16)
    return high, (value - high.astype(F32)).astype(BF16)


def thirds(value):
    parts = []
    for _ in range(3):
        part = value.astype(F8)
        parts.append(part)
        value = (value - part.astype(F32)) * 16.0
    return jnp.concatenate(parts, axis=0)


def dot(a, b):
    return jnp.dot(a, b, preferred_element_type=F32)


def body(
    n_mem,
    n_lat,
    cells_ref,
    count_ref,
    innov_ref,
    scale_ref,
    pert_ref,
    sel_ref,
    win_ref,
    widen_ref,
    control_ref,
    inc_ref,
    meta,
    bvals,
    spread,
    chosen,
    picked,
    onehot,
    onehot8,
    filt,
    filt2,
    target,
    scale,
    live,
    observed,
    summed,
    q_now,
    weight,
    acc,
    vext,
    vwide,
    along,
    image,
    image_acc,
    hsend,
    hrecv,
    hnear,
    ssend,
    srecv,
    irecv,
    meta_send,
    meta_recv,
    b_send,
    b_recv,
    h_send,
    h_recv,
    n_send,
    n_recv,
    s_send,
    s_recv,
    i_send,
    i_recv,
):
    members, fine_rows, fine_cols = pert_ref.shape
    rows, cols = fine_rows // 2, fine_cols // 2
    slots = cells_ref.shape[1]
    flat = members * rows
    c = float((members * n_mem - 1) ** -0.5)
    mem = lax.axis_index("mem")
    lat = lax.axis_index("lat")
    barrier = pltpu.get_barrier_semaphore()

    def mem_peer(r):
        return {"mem": lax.rem(mem + r, n_mem)}

    def lat_peer(r):
        return {"lat": lax.rem(lat + r, n_lat)}

    def offset(n):
        return ((n + 1) // 2) * (1 - 2 * (n % 2))

    def remote(src, dst, send, recv, device):
        return pltpu.make_async_remote_copy(
            src_ref=src,
            dst_ref=dst,
            send_sem=send,
            recv_sem=recv,
            device_id=device,
            device_id_type=MESH,
        )

    def wait_all(ref, sem):
        pltpu.make_async_copy(ref, ref, sem).wait()

    @pl.loop(1, n_mem)
    def _(r):
        pl.semaphore_signal(barrier, inc=1, device_id=mem_peer(r), device_id_type=MESH)

    @pl.loop(1, n_lat)
    def _(r):
        pl.semaphore_signal(barrier, inc=1, device_id=lat_peer(r), device_id_type=MESH)

    cells = cells_ref[...]
    slot_id = lax.broadcasted_iota(jnp.int32, (1, slots), 1)
    meta[0, 0:1, :] = cells.astype(F32)
    meta[0, 1:2, :] = innov_ref[...]
    meta[0, 2:3, :] = scale_ref[...]
    meta[0, 3:4, :] = jnp.where(slot_id < count_ref[0], 1.0, 0.0)

    def place_of(n, at):
        cell = meta[n, 0:1, at]
        fine_row = jnp.floor(cell * (1.0 / fine_cols))
        return fine_row, cell - fine_row * float(fine_cols)

    def near_peer(n):
        return {"lat": lax.rem(lat - offset(n) + n_lat, n_lat)}

    def meta_copy(n):
        return remote(
            meta.at[0], meta.at[n], meta_send.at[n - 1], meta_recv.at[n - 1], near_peer(n)
        )

    def value_copy(n):
        return remote(
            bvals.at[0], bvals.at[n], b_send.at[n - 1], b_recv.at[n - 1], near_peer(n)
        )

    @pl.loop(0, fine_cols // BLOCK)
    def _(j):
        at = pl.ds(pl.multiple_of(j * BLOCK, BLOCK), BLOCK)
        picked[:, at] = dot(
            sel_ref[...], pert_ref[:, :, at].reshape(members * fine_rows, BLOCK)
        ).astype(BF16)

    @pl.loop(0, slots // BLOCK)
    def _(j):
        at = pl.ds(pl.multiple_of(j * BLOCK, BLOCK), BLOCK)
        fine_row, column = place_of(0, at)
        coarse_row = jnp.floor(fine_row * 0.5)
        place = lax.broadcasted_iota(jnp.int32, (fine_cols, BLOCK), 0).astype(F32)
        hit = jnp.where(place == column, 1.0, 0.0).astype(BF16)
        both = dot(picked[...], hit)
        odd = fine_row - 2.0 * coarse_row
        value = jnp.where(odd > 0.5, both[flat:], both[:flat])
        own = lax.broadcasted_iota(jnp.int32, (rows, BLOCK), 0).astype(F32) == coarse_row
        value = jnp.where(own[None], value.reshape(members, rows, BLOCK), 0.0)
        chosen[:, at] = value.reshape(flat, BLOCK).astype(BF16)
        bvals[0, :, at] = jnp.sum(value, axis=1)

    target[...] = jnp.zeros_like(target)
    scale[...] = jnp.ones_like(scale)
    live[...] = jnp.zeros_like(live)
    observed[...] = jnp.zeros_like(observed)
    summed[...] = jnp.zeros_like(summed)

    def prepare(n):
        fine_row, column = place_of(n, slice(None))
        x = column * 0.5
        step = 128
        place16 = lax.broadcasted_iota(jnp.int32, (step, slots), 0).astype(F32).astype(BF16)

        @pl.loop(0, cols // step)
        def _(j):
            start = pl.multiple_of(j * step, step)
            near = jnp.clip(x - start.astype(F32), -2.0, step + 1.0).astype(BF16)
            hat = jnp.maximum(BF16(1.0) - jnp.abs(near - place16), BF16(0.0))
            onehot8[n, pl.ds(start, step), :] = hat.astype(F8)

            @pl.when(n == 0)
            def _():
                onehot[pl.ds(start, step), :] = hat

        place = lax.broadcasted_iota(jnp.int32, (32, slots), 0).astype(F32)
        hat = jnp.maximum(
            jnp.maximum(1.0 - jnp.abs(x - place), 1.0 - jnp.abs(x - (place + float(cols)))), 0.0
        )
        onehot8[n, 0:32, :] = hat.astype(F8)

        @pl.when(n == 0)
        def _():
            onehot[0:32, :] = hat.astype(BF16)

        reach = rows + 2 * HALO
        between = lax.broadcasted_iota(jnp.int32, (reach, slots), 0) - HALO
        whole = between + lat * rows
        shift = jnp.asarray(offset(n) * rows, jnp.int32).astype(F32)
        apart = between.astype(F32) - (jnp.floor(fine_row * 0.5) + shift)
        spread_sq = 2.0 * (HALO / 2.0) ** 2
        taps = jnp.where(
            (jnp.abs(apart) <= HALO) & (whole >= 0) & (whole < n_lat * rows),
            (0.5 * c) * jnp.exp(-apart * apart / spread_sq),
            0.0,
        )
        filt[n] = taps[HALO : HALO + rows]
        own = lax.broadcasted_iota(jnp.int32, (rows, reach), 0).astype(F32)
        middle = lax.broadcasted_iota(jnp.int32, (rows, reach), 1).astype(F32) - HALO
        away = middle - own
        first = jnp.where(jnp.abs(away) <= HALO, 0.5 * jnp.exp(-away * away / spread_sq), 0.0)
        filt2[n] = jnp.dot(
            first, taps, precision=lax.Precision.HIGHEST, preferred_element_type=F32
        )
        band = lat + offset(n)
        inside = jnp.where((band >= 0) & (band < n_lat), 1.0, 0.0)
        target[pl.ds(n, 1), :] = meta[n, 1:2, :]
        scale[pl.ds(n, 1), :] = meta[n, 2:3, :]
        live[pl.ds(n, 1), :] = meta[n, 3:4, :] * inside

    pl.semaphore_wait(barrier, n_mem + n_lat - 2)

    @pl.loop(1, NEAR)
    def _(n):
        meta_copy(n).start()

    @pl.loop(1, 3)
    def _(n):
        value_copy(n).start()

    @pl.loop(0, NEAR)
    def _(n):
        @pl.when(n > 0)
        def _():
            meta_copy(n).wait_recv()

        @pl.when(n == 1)
        def _():
            value_copy(3).start()
            value_copy(4).start()

        prepare(n)

    image_acc[...] = jnp.zeros_like(image_acc)
    control_ref[...] = jnp.zeros_like(control_ref)

    def scattered(filter_ref, bands, first):
        acc[...] = jnp.zeros_like(acc)
        peak = jnp.max(jnp.max(jnp.abs(q_now[...]), axis=0, keepdims=True), axis=1, keepdims=True)
        peak = jnp.maximum(peak, 1e-30)
        gain = (ROOM / c) / peak

        @pl.loop(0, bands)
        def _(n):
            @pl.when(first & (n > 0))
            def _():
                value_copy(n).wait_recv()

            @pl.when(first)
            def _():
                values = jnp.broadcast_to(bvals[n][:, None, :], (members, rows, slots))
                spread[n] = values.reshape(flat, slots).astype(BF16)

            factor = filter_ref[n] * (q_now[pl.ds(n, 1), :] * gain)
            value = spread[n].astype(F32).reshape(members, rows, slots) * factor[None]
            acc[...] += lax.dot_general(
                thirds(value.reshape(flat, slots)),
                onehot8[n],
                (((1,), (1,)), ((), ())),
                preferred_element_type=F32,
            )

        total = acc[:flat] + (1.0 / 16.0) * (acc[flat : 2 * flat] + (1.0 / 16.0) * acc[2 * flat :])
        return total * (peak * (c / ROOM))

    def filtered(value, which):
        high, low = halves(value)
        both = jnp.concatenate([high, low], axis=0)
        vext[:, PAD : PAD + cols] = both
        vext[:, :PAD] = both[:, cols - PAD :]
        vext[:, PAD + cols :] = both[:, :PAD]
        blocks = []
        for j in range(cols // BLOCK):
            window = vext[:, j * BLOCK : j * BLOCK + BLOCK + 2 * PAD]
            product = dot(window, win_ref[2 * which])
            blocks.append(
                product[:flat] + product[flat:] + dot(window[:flat], win_ref[2 * which + 1])
            )
        return blocks

    def send_image(k):
        @pl.loop(1, n_mem)
        def _(r):
            to = lax.rem(mem + r, n_mem)
            width = inc_ref.shape[1]
            part = pl.ds(pl.multiple_of(to * width, 128), width)
            remote(
                image.at[k, :, part], irecv.at[k, r - 1], i_send.at[k], i_recv.at[k], mem_peer(r)
            ).start()

    @pl.loop(0, ITERS)
    def _(t):
        last = t == ITERS - 1
        bounded = jnp.tanh((target[...] - observed[...]) / scale[...])
        q_now[...] = live[...] * (scale[...] * bounded) - summed[...]
        weight[...] = (live[...] * (1.0 - bounded * bounded))[0:1]

        for j, block in enumerate(filtered(scattered(filt2, NEAR, t == 0), 1)):
            high, low = halves(block)
            vwide[:, j * BLOCK : (j + 1) * BLOCK] = jnp.concatenate([high, low], axis=0)
        vwide[:, cols:] = vwide[:, :PAD]

        seen = dot(vwide[:, :cols], onehot[...])
        hits_part = c * jnp.sum(
            chosen[...].astype(F32) * (seen[:flat] + seen[flat:]), axis=0, keepdims=True
        )
        hsend[t] = hits_part

        @pl.loop(1, n_mem)
        def _(r):
            remote(
                hsend.at[t], hrecv.at[t, r - 1], h_send.at[t], h_recv.at[t], mem_peer(r)
            ).start()

        at_t = jnp.where(last, 1, 0)
        for j in range(fine_cols // 256):
            wide = dot(vwide[:, 128 * j : 128 * j + 256], widen_ref[...])
            wide = (wide[:flat] + wide[flat:]).reshape(members, rows, 256)
            here = slice(256 * j, 256 * (j + 1))
            for e in range(2):
                pert = picked[e * flat : (e + 1) * flat, here].astype(F32)
                total = c * jnp.sum(pert.reshape(members, rows, 256) * wide, axis=0)
                image[at_t, e * rows : (e + 1) * rows, here] = total

        @pl.when(last)
        def _():
            send_image(1)

        wait_all(hrecv.at[t], h_recv.at[t])
        hits = hits_part + jnp.sum(hrecv[t], axis=0)
        q_own = q_now[0:1, :]
        gg_part = q_own * hits
        cc_part = weight[...] * hits * hits
        width = 128
        ssend[t, :, :width] = sum(
            gg_part[:, i : i + width] for i in range(0, slots, width)
        )
        ssend[t, :, width:] = sum(
            cc_part[:, i : i + width] for i in range(0, slots, width)
        )

        @pl.loop(1, n_lat)
        def _(r):
            remote(
                ssend.at[t], srecv.at[t, r - 1], s_send.at[t], s_recv.at[t], lat_peer(r)
            ).start()

        @pl.when(jnp.logical_not(last))
        def _():
            hnear[t, 0] = hits

        def near_hits(n):
            return remote(
                hnear.at[t, 0],
                hnear.at[t, n],
                n_send.at[t, n - 1],
                n_recv.at[t, n - 1],
                near_peer(n),
            )

        @pl.when(jnp.logical_not(last))
        def _():
            @pl.loop(1, NEAR)
            def _(n):
                near_hits(n).start()

        for j, block in enumerate(filtered(scattered(filt, 3, t < 0), 0)):
            along[:, j * BLOCK : (j + 1) * BLOCK] = block

        wait_all(srecv.at[t], s_recv.at[t])
        sums = ssend[t] + jnp.sum(srecv[t], axis=0)
        gg = jnp.maximum(jnp.sum(sums[:, :width], axis=1, keepdims=True), 0.0)
        cc = jnp.sum(sums[:, width:], axis=1, keepdims=True)
        step = gg / (gg + cc + 1e-6)

        control_ref[...] += step[None] * along[...].reshape(members, rows, cols)
        summed[...] += step * q_now[...]
        observed[0:1, :] += step * hits

        @pl.when(jnp.logical_not(last))
        def _():
            @pl.loop(1, NEAR)
            def _(n):
                near_hits(n).wait_recv()
                observed[pl.ds(n, 1), :] += step * hnear[t, n]

            image_acc[...] += step * image[0]

        @pl.when(t == ITERS - 2)
        def _():
            image[0] = image_acc[...]
            send_image(0)

        @pl.when(last)
        def _():
            width = inc_ref.shape[1]
            part = pl.ds(pl.multiple_of(mem * width, 128), width)
            wait_all(irecv.at[0], i_recv.at[0])
            wait_all(irecv.at[1], i_recv.at[1])
            before = image[0, :, part] + jnp.sum(irecv[0], axis=0)
            now = image[1, :, part] + jnp.sum(irecv[1], axis=0)
            total = before + step * now
            for e in range(2):
                inc_ref[pl.ds(e, rows, 2), :] = total[e * rows : (e + 1) * rows]

    @pl.loop(1, NEAR)
    def _(n):
        meta_copy(n).wait_send()
        value_copy(n).wait_send()

    @pl.loop(0, ITERS)
    def _(t):
        wait_all(hrecv.at[t], h_send.at[t])
        wait_all(srecv.at[t], s_send.at[t])

        @pl.when(t < ITERS - 1)
        def _():
            @pl.loop(1, NEAR)
            def _(n):
                wait_all(hnear.at[t, n], n_send.at[t, n - 1])

    wait_all(irecv.at[0], i_send.at[0])
    wait_all(irecv.at[1], i_send.at[1])


def on_device(n_mem, n_lat, windows, pert, cells, count, innov, scale):
    members, fine_rows, fine_cols = pert.shape
    rows, cols = fine_rows // 2, fine_cols // 2
    slots = cells.shape[1]
    flat = members * rows
    width = fine_cols // n_mem
    vmem = pl.BlockSpec(memory_space=pltpu.VMEM)
    scratch = [
        pltpu.VMEM((NEAR, 4, slots), F32),
        pltpu.VMEM((NEAR, members, slots), F32),
        pltpu.VMEM((NEAR, flat, slots), BF16),
        pltpu.VMEM((flat, slots), BF16),
        pltpu.VMEM((2 * flat, fine_cols), BF16),
        pltpu.VMEM((cols, slots), BF16),
        pltpu.VMEM((NEAR, cols, slots), F8),
        pltpu.VMEM((NEAR, rows, slots), F32),
        pltpu.VMEM((NEAR, rows, slots), F32),
        pltpu.VMEM((8, slots), F32),
        pltpu.VMEM((8, slots), F32),
        pltpu.VMEM((8, slots), F32),
        pltpu.VMEM((8, slots), F32),
        pltpu.VMEM((8, slots), F32),
        pltpu.VMEM((8, slots), F32),
        pltpu.VMEM((1, slots), F32),
        pltpu.VMEM((3 * flat, cols), F32),
        pltpu.VMEM((2 * flat, cols + 2 * PAD), BF16),
        pltpu.VMEM((2 * flat, cols + PAD), BF16),
        pltpu.VMEM((flat, cols), F32),
        pltpu.VMEM((2, fine_rows, fine_cols), F32),
        pltpu.VMEM((fine_rows, fine_cols), F32),
        pltpu.VMEM((ITERS, 1, slots), F32),
        pltpu.VMEM((ITERS, n_mem - 1, 1, slots), F32),
        pltpu.VMEM((ITERS - 1, NEAR, 1, slots), F32),
        pltpu.VMEM((ITERS, 1, 256), F32),
        pltpu.VMEM((ITERS, n_lat - 1, 1, 256), F32),
        pltpu.VMEM((2, n_mem - 1, fine_rows, width), F32),
    ]
    scratch += [pltpu.SemaphoreType.DMA((NEAR - 1,))] * 4
    scratch += [pltpu.SemaphoreType.DMA((ITERS,))] * 2
    scratch += [pltpu.SemaphoreType.DMA((ITERS - 1, NEAR - 1))] * 2
    scratch += [pltpu.SemaphoreType.DMA((ITERS,))] * 2
    scratch += [pltpu.SemaphoreType.DMA((2,))] * 2
    control, increment = pl.pallas_call(
        functools.partial(body, n_mem, n_lat),
        out_shape=(
            jax.ShapeDtypeStruct((members, rows, cols), F32),
            jax.ShapeDtypeStruct((fine_rows, width), F32),
        ),
        in_specs=[vmem, pl.BlockSpec(memory_space=pltpu.SMEM)] + [vmem] * 6,
        out_specs=(vmem, vmem),
        scratch_shapes=scratch,
        compiler_params=pltpu.CompilerParams(
            collective_id=0, has_side_effects=True, vmem_limit_bytes=60 * 2**20
        ),
    )(
        cells,
        count,
        innov,
        scale,
        pert,
        jnp.asarray(split_rows_matrix(members, fine_rows)),
        jnp.asarray(windows),
        jnp.asarray(widen_matrix()),
    )
    return control, increment


def solution(mesh):
    n_mem, n_lat = mesh.shape["mem"], mesh.shape["lat"]

    def run(pert, cells, count, innov, scale):
        windows = window_matrices(pert.shape[2] // 2)
        return on_device(n_mem, n_lat, windows, pert, cells, count, innov, scale)

    return jax.shard_map(
        run,
        mesh=mesh,
        in_specs=(P("mem", "lat", None), P("lat", None), P("lat"), P("lat", None), P("lat", None)),
        out_specs=(P("mem", "lat", None), P("lat", "mem")),
        check_vma=False,
    )
```
